512 devices in a mesh: wide: 64 (over z, y_hi, core), narrow: 8 (over x, y_lo).
Axes of the slice: x: 4, y: 4 (y_hi: 2, y_lo: 2; y = y_hi * 2 + y_lo), z: 16, core: 2. Of those that a mesh axis runs over, the one named last changes fastest.
Arguments:
- points: float32 [32, 98304], P(None, ('wide', 'narrow')), may hold values from -6 to 6
- lengthscale: float32 [32], replicated, may hold values from 2.5 to 8
- noise: float32 [1], replicated, may hold values from 1 to 16
- direction: float32 [32, 98304], P(None, ('wide', 'narrow')), may hold values from -10.8 to 10.8
- residual: float32 [32, 98304], P(None, ('wide', 'narrow')), may hold values from -10.8 to 10.8
- solution: float32 [32, 98304], P(None, ('wide', 'narrow')), may hold values from -6 to 6
Outputs:
- new_solution: float32 [32, 98304], P(None, ('wide', 'narrow'))
- new_residual: float32 [32, 98304], P(None, ('wide', 'narrow'))
- new_direction: float32 [32, 98304], P(None, ('wide', 'narrow'))
- norm_sq: float32 [32], replicated
The draws below stay inside these ranges and needn't reach their ends.
All inputs are finite; a program needn't handle non-finite values.
Results may differ from the reference program's by a relative error of at most 0.0024.
Values may be sent and summed in bfloat16 or wider, within the bound.
A program may use at most 64 MiB of HBM per device.

```python
import math
import jax
import jax.numpy as jnp
from jax import lax

DIN = 32
NCOL = 32
NPTS = 98304


def shape_scales(base, key_col, key_row):
    col_scale = jnp.exp(jnp.log(10.0) * (jax.random.uniform(key_col, (NCOL, 1), jnp.float32) - 1.0))
    place = jnp.arange(NPTS, dtype=jnp.float32) / NPTS
    row_scale = jnp.exp(jnp.log(3.0) * place)[None, :] * jnp.exp(jnp.log(3.0) * jax.random.uniform(key_row, (1, NPTS), jnp.float32))
    return base * col_scale * row_scale * 0.3


def draw_residual(key, part):
    key = jax.random.fold_in(key, 11)
    key_base, key_col, key_row = jax.random.split(key, 3)
    base = jnp.clip(jax.random.normal(key_base, (NCOL, NPTS), jnp.float32), -4.0, 4.0)
    return shape_scales(base, key_col, key_row)


def draw_direction(key, part):
    key = jax.random.fold_in(key, 12)
    key_base, key_col, key_row = jax.random.split(key, 3)
    base = jnp.clip(jax.random.normal(key_base, (NCOL, NPTS), jnp.float32), -4.0, 4.0)
    return shape_scales(base, key_col, key_row)


def levels(own_key, extent, shards, least, largest):
    def one(position, shards_of):
        steps = jax.random.uniform(jax.random.fold_in(jax.random.fold_in(own_key, 6), position), (shards_of,), jnp.float32, least / len(shards), largest / len(shards))
        return jnp.repeat(jnp.exp(steps), extent[position] // shards_of).reshape((-1,) + (1,) * (len(extent) - position - 1))

    loudness = one(*shards[0])
    for cut in shards[1:]:
        loudness = loudness * one(*cut)
    return loudness


def gaussian(key, shape, width, reach, cuts=(), kind=jnp.bfloat16):
    values = width * jax.random.normal(key, shape, jnp.float32)
    if cuts:
        values = values * levels(key, shape, cuts, -0.22, 0.18)
    return jnp.clip(values, -reach, reach).astype(kind)


def setup_inputs(seed: int = 0) -> dict:
    keys = jax.random.split(jax.random.key(seed), 7)
    return {
        "points": gaussian(keys[0], (DIN, NPTS), 1.0, 6.0, ((1, 512),), jnp.float32),
        "lengthscale": jnp.clip(jnp.exp(jax.random.uniform(keys[1], (DIN,), jnp.float32, math.log(2.5), math.log(8.0))), 2.5, 8.0),
        "noise": jnp.clip(jnp.exp(jax.random.uniform(keys[2], (1,), jnp.float32, math.log(1.0), math.log(16.0))), 1.0, 16.0),
        "direction": draw_direction(jax.random.fold_in(keys[6], 71), 0),
        "residual": draw_residual(jax.random.fold_in(keys[6], 71), 0),
        "solution": gaussian(keys[5], (NCOL, NPTS), 1.0, 6.0, ((1, 512),), jnp.float32),
    }


def kernel_tile(home_s, home_n, vis_s):
    cross = lax.dot_general(home_s, vis_s, (((0,), (0,)), ((), ())), precision=lax.Precision.HIGHEST, preferred_element_type=jnp.float32)
    vis_n = lax.optimization_barrier(jnp.sum(vis_s * vis_s, axis=0))
    dist_sq = home_n[:, None] + vis_n[None, :] - 2.0 * cross
    radius = jnp.sqrt(5.0 * jnp.maximum(dist_sq, 0.0))
    return ((1.0 + radius + radius * radius / 3.0) * jnp.exp(-radius)).astype(jnp.bfloat16)

def reference(points, lengthscale, noise, direction, residual, solution):
    scaled = points / lengthscale[:, None]
    dir_bf = direction.astype(jnp.bfloat16)
    row_blk = math.gcd(NPTS, 1024)
    col_blk = math.gcd(NPTS, 8192)
    nrows = NPTS // row_blk
    ncols = NPTS // col_blk
    col_pts = scaled.reshape(DIN, ncols, col_blk).transpose(1, 0, 2)
    col_dirs = dir_bf.reshape(NCOL, ncols, col_blk).transpose(1, 0, 2)

    def row_block(index):
        home_s = lax.dynamic_slice_in_dim(scaled, index * row_blk, row_blk, 1)
        home_n = lax.optimization_barrier(jnp.sum(home_s * home_s, axis=0))

        def visit(total, item):
            tile = kernel_tile(home_s, home_n, item[0])
            part = lax.dot_general(item[1], tile, (((1,), (1,)), ((), ())), preferred_element_type=jnp.float32)
            return (total + part, None)
        start = jnp.zeros((NCOL, row_blk), jnp.float32)
        return lax.scan(visit, start, (col_pts, col_dirs))[0]
    blocks = lax.map(row_block, jnp.arange(nrows, dtype=jnp.int32))
    kernel_dir = blocks.transpose(1, 0, 2).reshape(NCOL, NPTS) + noise[0] * direction
    resid_sq = lax.optimization_barrier(jnp.sum(residual * residual, axis=1))
    curve = lax.optimization_barrier(jnp.sum(direction * kernel_dir, axis=1))
    alpha = resid_sq / curve
    new_solution = solution + alpha[:, None] * direction
    new_residual = residual - alpha[:, None] * kernel_dir
    norm_sq = lax.optimization_barrier(jnp.sum(new_residual * new_residual, axis=1))
    new_direction = new_residual + (norm_sq / resid_sq)[:, None] * direction
    return (new_solution, new_residual, new_direction, norm_sq)
```

```python
import functools
import math

import jax
import jax.numpy as jnp
from jax import lax
from jax.experimental import pallas as pl
from jax.experimental.pallas import tpu as pltpu
from jax.sharding import PartitionSpec as P

F32, BF16 = jnp.float32, jnp.bfloat16
MESH = pl.DeviceIdType.MESH
NX, NY, NZ = 4, 4, 16
NPEER = NX * NY
BLK = 192
CHUNK = NY * BLK
HOME = NPEER * BLK
VIS = 2 * BLK
HALF = NZ // 2
COORD_SCALE = math.sqrt(5.0) / 3.0
EXP_SCALE = -3.0 * math.log2(math.e)
EXP_SHIFT = math.log2(3.0)
NT = (((1,), (1,)), ((), ()))


def matern(u):
    u = jnp.maximum(u, 1e-30)
    q = u * lax.rsqrt(u)
    e = jnp.exp2(q * EXP_SCALE + EXP_SHIFT)
    return (((u + q) + (1.0 / 3.0)) * e).astype(BF16)


def pack_tail(tail):
    lane = lax.broadcasted_iota(jnp.int32, (16, 128), 1)
    return jnp.where(lane < 64, tail[0:16], pltpu.roll(tail[16:32], 64, 1))


def unpack_tails(a, b):
    lane = lax.broadcasted_iota(jnp.int32, (16, 128), 1)
    top = jnp.where(lane < 64, a, pltpu.roll(b, 64, 1))
    bottom = jnp.where(lane < 64, pltpu.roll(a, 64, 1), b)
    return jnp.concatenate([top, bottom], axis=0)


def unpack(blocks):
    heads = [b[0:32] for b in blocks]
    tails = [unpack_tails(blocks[i][32:48], blocks[i + 1][32:48]) for i in range(0, len(blocks), 2)]
    return jnp.concatenate(heads + tails, axis=1)


def split3(v):
    hi = v.astype(BF16)
    rest = v - hi.astype(F32)
    mid = rest.astype(BF16)
    lo = (rest - mid.astype(F32)).astype(BF16)
    return hi, mid, lo


def norm_rows(s, first):
    sq = jnp.sum(s * s, axis=0, keepdims=True)
    hi, mid, lo = (p.astype(F32) for p in split3(sq))
    row = lax.broadcasted_iota(jnp.int32, (16, s.shape[1]), 0)
    ones = jnp.where(row < 6, 1.0, 0.0)
    rows = jnp.where(row == first, hi, jnp.where(row == first + 1, mid, jnp.where(row == first + 2, lo, ones)))
    return rows.astype(BF16)


def home_operand(s):
    hi, mid, lo = split3(s)
    pad = jnp.zeros((48, s.shape[1]), BF16)
    return jnp.concatenate([hi, hi, mid, mid, hi, lo, norm_rows(s, 0), pad], axis=0)


def visitor_operand(s):
    hi, mid, lo = split3(s)
    hi, mid, lo = (p * BF16(-2.0) for p in (hi, mid, lo))
    pad = jnp.zeros((48, s.shape[1]), BF16)
    return jnp.concatenate([hi, mid, hi, mid, lo, hi, norm_rows(s, 3), pad], axis=0).T


def to_row(cols):
    lane = lax.broadcasted_iota(jnp.int32, (32, 128), 1)
    sub = lax.broadcasted_iota(jnp.int32, (32, 128), 0)
    out = jnp.zeros((32, 128), F32)
    for i, col in enumerate(cols):
        out = jnp.where(lane == sub + 32 * i, col, out)
    return jnp.sum(out, axis=0, keepdims=True)


def to_col(row, i):
    lane = lax.broadcasted_iota(jnp.int32, (32, 128), 1)
    sub = lax.broadcasted_iota(jnp.int32, (32, 128), 0)
    return jnp.sum(jnp.where(lane == sub + 32 * i, row, 0.0), axis=1, keepdims=True)


def kernel(
    pts_ref, ls_ref, noise_ref, dir_ref, res_ref, sol_ref,
    sol_out, res_out, dir_out, norm_out,
    tail, own_s, own_d, home_s, home_d, vis_s, vis_d, hb, hd, va, vd, hacc, vacc,
    chain, fin_a, fin_b, red_a, red_b, ar1_src, ar1, ar2_src, ar2, ar3_src, ar3,
    home_send, home_recv, zs_send, z_recv, sib_send, sib_recv, ch_send, ch_recv,
    fin_send, fin_recv, red_send, red_recv, ar1_send, ar1_recv, ar2_send, ar2_recv, ar3_send, ar3_recv,
):
    wide, narrow = lax.axis_index("wide"), lax.axis_index("narrow")
    z, y_hi, core = wide // 4, (wide // 2) % 2, wide % 2
    x, y_lo = narrow // 2, narrow % 2
    y = y_hi * 2 + y_lo

    def peer(dz=0, dx=0, dy=0, dc=0):
        pz, px, py, pc = (z + dz) % NZ, (x + dx) % NX, (y + dy) % NY, (core + dc) % 2
        return (pz * 4 + (py // 2) * 2 + pc, px * 2 + py % 2)

    def remote(src, dst, send, recv, dev):
        return pltpu.make_async_remote_copy(
            src_ref=src, dst_ref=dst, send_sem=send, recv_sem=recv, device_id=dev, device_id_type=MESH
        )

    plane = [(dx, dy) for dx in range(NX) for dy in range(NY)]

    barrier = pltpu.get_barrier_semaphore()
    for dx, dy in plane[1:]:
        pl.semaphore_signal(barrier, inc=1, device_id=peer(dx=dx, dy=dy), device_id_type=MESH)
    for dz in range(1, NZ):
        pl.semaphore_signal(barrier, inc=1, device_id=peer(dz=dz), device_id_type=MESH)
    pl.semaphore_signal(barrier, inc=1, device_id=peer(dc=1), device_id_type=MESH)
    pl.semaphore_signal(barrier, inc=1, device_id=peer(dz=NZ - (HALF - 1), dc=1), device_id_type=MESH)

    eye = lax.broadcasted_iota(jnp.int32, (32, 32), 0) == lax.broadcasted_iota(jnp.int32, (32, 32), 1)
    scale = jnp.sum(jnp.where(eye, ls_ref[...], 0.0), axis=1, keepdims=True)
    scaled = pts_ref[...] / scale * COORD_SCALE
    own_s[0:32] = scaled[:, 0:128]
    tail[...] = jnp.zeros_like(tail)
    tail[:, 0:64] = scaled[:, 128:192]
    own_s[32:48] = pack_tail(tail[...])
    own_d[0:32] = dir_ref[:, 0:128].astype(BF16)
    tail[:, 0:64] = dir_ref[:, 128:192]
    own_d[32:48] = pack_tail(tail[...]).astype(BF16)
    hacc[...] = jnp.zeros_like(hacc)

    pl.semaphore_wait(barrier, 2 + NZ - 1 + NPEER - 1)

    def home_copy(i, which):
        dx, dy = plane[i]
        back = plane.index(((-dx) % NX, (-dy) % NY))
        src, dst = ((own_s, home_s), (own_d, home_d))[which]
        return remote(src, dst.at[back], home_send.at[which, i], home_recv.at[which, back], peer(dx=dx, dy=dy))

    def z_copy(k, which):
        src, dst = ((vis_s, vis_d))[which], ((vis_s, vis_d))[which]
        return remote(src.at[k, 0], dst.at[k + 1, 0], zs_send.at[which, k], z_recv.at[which, k + 1], peer(dz=NZ - 1))

    def sib_copy(k, which):
        buf = (vis_s, vis_d)[which]
        return remote(buf.at[k, 0], buf.at[k, 1], sib_send.at[which, k], sib_recv.at[which, k], peer(dc=1))

    vis_s[0, 0] = own_s[...]
    vis_d[0, 0] = own_d[...]
    for which in range(2):
        z_copy(0, which).start()
        sib_copy(0, which).start()
    for i in range(1, NPEER):
        for which in range(2):
            home_copy(i, which).start()

    def set_visitors(k):
        va[...] = visitor_operand(unpack([vis_s[k, 0], vis_s[k, 1]]))
        vd[...] = unpack([vis_d[k, 0].astype(F32), vis_d[k, 1].astype(F32)]).astype(BF16)

    def arrived(k):
        for which in range(2):
            z_copy(k - 1, which).wait_recv()
        for which in range(2):
            sib_copy(k, which).start()

    for which in range(2):
        sib_copy(0, which).wait_recv()
    set_visitors(0)
    home_s[0] = own_s[...]
    home_d[0] = own_d[...]
    for g in range(NX):
        for i in range(4 * g, 4 * g + 4):
            if i:
                for which in range(2):
                    home_copy(plane.index(((-plane[i][0]) % NX, (-plane[i][1]) % NY)), which).wait_recv()
        cols = pl.ds(g * CHUNK, CHUNK)
        hb[:, cols] = home_operand(unpack([home_s[i] for i in range(4 * g, 4 * g + 4)]))
        hd[:, cols] = unpack([home_d[i].astype(F32) for i in range(4 * g, 4 * g + 4)]).astype(BF16)

    def tile(cols):
        return matern(jnp.dot(va[...], hb[:, cols], preferred_element_type=F32))

    def home_only(t, carry):
        cols = pl.ds(pl.multiple_of(t * CHUNK, CHUNK), CHUNK)
        hacc[:, cols] += jnp.dot(vd[...], tile(cols), preferred_element_type=F32)
        return carry

    lax.fori_loop(0, NX, home_only, 0)

    arrived(1)
    for which in range(2):
        z_copy(1, which).start()

    def both(k, carry):
        arrived(k + 1)

        @pl.when(k < HALF - 1)
        def _():
            for which in range(2):
                z_copy(k + 1, which).start()

        for which in range(2):
            sib_copy(k, which).wait_recv()
        set_visitors(k)
        vacc[...] = jnp.zeros_like(vacc)

        def one(t, inner):
            cols = pl.ds(pl.multiple_of(t * 2 * CHUNK, 2 * CHUNK), 2 * CHUNK)
            k_tile = tile(cols)
            hacc[:, cols] += jnp.dot(vd[...], k_tile, preferred_element_type=F32)
            vacc[...] += lax.dot_general(hd[:, cols], k_tile, NT, preferred_element_type=F32)
            return inner

        lax.fori_loop(0, NX // 2, one, 0)

        @pl.when(k == 1)
        def _():
            chain[k] = vacc[...]

        @pl.when(k > 1)
        def _():
            chain_copy(k - 1).wait_recv()
            chain[k] += vacc[...]

        @pl.when(k < HALF - 1)
        def _():
            chain_copy(k).start()

        return carry

    def chain_copy(k):
        return remote(chain.at[k], chain.at[k + 1], ch_send.at[k], ch_recv.at[k + 1], peer(dz=NZ - 1))

    lax.fori_loop(1, HALF, both, 0)

    def fin_copy(f, part):
        src = chain.at[HALF - 1, :, pl.ds(128 * f, 128)] if part == 0 else chain.at[HALF - 1, :, pl.ds(256, 128)]
        dst = (fin_a, fin_b)[part].at[f]
        return remote(src, dst, fin_send.at[f, part], fin_recv.at[f, part], peer(dz=HALF - 1, dc=f))

    for f in range(2):
        for part in range(2):
            fin_copy(f, part).start()

    for which in range(2):
        sib_copy(HALF, which).wait_recv()
    set_visitors(HALF)

    def red_copy(i, part):
        dx, dy = plane[i]
        back = plane.index(((-dx) % NX, (-dy) % NY))
        base = dx * CHUNK + (128 * dy if part == 0 else 512 + 128 * (dy // 2))
        src = hacc.at[:, pl.ds(base, 128)]
        dst = (red_a, red_b)[part].at[back]
        return remote(src, dst, red_send.at[part, i], red_recv.at[part, back], peer(dx=dx, dy=dy))

    for g in (1, 2, 3, 0):
        home_only(g, 0)
        for i in range(4 * g, 4 * g + 4):
            if i:
                for part in range(2):
                    red_copy(i, part).start()

    sum_a = hacc[:, 0:128]
    even, odd = hacc[:, 512:640], jnp.zeros((32, 128), F32)
    for f in range(2):
        for part in range(2):
            fin_copy(f, part).wait_recv()
    sum_a = sum_a + fin_a[0] + fin_a[1]
    even = even + fin_b[0]
    odd = odd + fin_b[1]
    for i in range(1, NPEER):
        back = plane.index(((-plane[i][0]) % NX, (-plane[i][1]) % NY))
        for part in range(2):
            red_copy(back, part).wait_recv()
        sum_a = sum_a + red_a[i]
        if i % 2:
            odd = odd + red_b[i]
        else:
            even = even + red_b[i]
    sum_b = even[:, 0:64] + pltpu.roll(odd, 64, 1)[:, 0:64]
    direction = dir_ref[...]
    residual = res_ref[...]
    kd = jnp.concatenate([sum_a, sum_b], axis=1) + noise_ref[0] * direction

    def total(v):
        return jnp.sum(v, axis=1, keepdims=True)

    sums = to_row([total(residual * residual), total(direction * kd), total(residual * kd), total(kd * kd)])

    ar1_src[...] = jnp.broadcast_to(sums, (8, 128))
    me1 = x * NY + y

    def ar1_copy(dx, dy, slot):
        return remote(ar1_src, ar1.at[slot], ar1_send.at[dx * NY + dy], ar1_recv.at[slot], peer(dx=dx, dy=dy))

    for dx, dy in plane[1:]:
        ar1_copy(dx, dy, me1).start()
    ar1[me1] = ar1_src[...]
    for dx, dy in plane[1:]:
        ar1_copy(dx, dy, ((x + dx) % NX) * NY + (y + dy) % NY).wait_recv()
    acc = ar1[0]
    for i in range(1, NPEER):
        acc = acc + ar1[i]
    ar2_src[...] = acc

    def ar2_copy(dz, slot):
        return remote(ar2_src, ar2.at[slot], ar2_send.at[dz], ar2_recv.at[slot], peer(dz=dz))

    for dz in range(1, NZ):
        ar2_copy(dz, z).start()
    ar2[z] = acc
    for dz in range(1, NZ):
        ar2_copy(dz, (z + dz) % NZ).wait_recv()
    acc = ar2[0]
    for i in range(1, NZ):
        acc = acc + ar2[i]
    ar3_src[...] = acc
    last = remote(ar3_src, ar3, ar3_send, ar3_recv, peer(dc=1))
    last.start()
    last.wait_recv()
    acc = (ar3_src[...] + ar3[...])[0:1]

    rr, curve, r_kd, kd_sq = (to_col(acc, i) for i in range(4))
    alpha = rr / curve
    norm_sq = rr - 2.0 * alpha * r_kd + alpha * alpha * kd_sq
    new_residual = residual - alpha * kd
    sol_out[...] = sol_ref[...] + alpha * direction
    res_out[...] = new_residual
    dir_out[...] = new_residual + (norm_sq / rr) * direction
    norm_out[...] = jnp.sum(jnp.where(eye, norm_sq, 0.0), axis=0, keepdims=True)

    for which in range(2):
        for k in range(HALF):
            z_copy(k, which).wait_send()
        for k in range(HALF + 1):
            sib_copy(k, which).wait_send()
        for i in range(1, NPEER):
            home_copy(i, which).wait_send()
            red_copy(i, which).wait_send()
    for k in range(1, HALF - 1):
        chain_copy(k).wait_send()
    for f in range(2):
        for part in range(2):
            fin_copy(f, part).wait_send()
    for dx, dy in plane[1:]:
        ar1_copy(dx, dy, me1).wait_send()
    for dz in range(1, NZ):
        ar2_copy(dz, z).wait_send()
    last.wait_send()


def body(points, lengthscale, noise, direction, residual, solution):
    vmem, smem = pl.BlockSpec(memory_space=pltpu.VMEM), pl.BlockSpec(memory_space=pltpu.SMEM)
    block = jax.ShapeDtypeStruct((32, BLK), F32)
    dma = pltpu.SemaphoreType.DMA
    out = pl.pallas_call(
        kernel,
        out_shape=[block, block, block, jax.ShapeDtypeStruct((1, 32), F32)],
        in_specs=[vmem, vmem, smem, vmem, vmem, vmem],
        out_specs=[vmem] * 4,
        scratch_shapes=[
            pltpu.VMEM((32, 128), F32),
            pltpu.VMEM((48, 128), F32),
            pltpu.VMEM((48, 128), BF16),
            pltpu.VMEM((NPEER, 48, 128), F32),
            pltpu.VMEM((NPEER, 48, 128), BF16),
            pltpu.VMEM((HALF + 1, 2, 48, 128), F32),
            pltpu.VMEM((HALF + 1, 2, 48, 128), BF16),
            pltpu.VMEM((256, HOME), BF16),
            pltpu.VMEM((32, HOME), BF16),
            pltpu.VMEM((VIS, 256), BF16),
            pltpu.VMEM((32, VIS), BF16),
            pltpu.VMEM((32, HOME), F32),
            pltpu.VMEM((32, VIS), F32),
            pltpu.VMEM((HALF, 32, VIS), F32),
            pltpu.VMEM((2, 32, 128), F32),
            pltpu.VMEM((2, 32, 128), F32),
            pltpu.VMEM((NPEER, 32, 128), F32),
            pltpu.VMEM((NPEER, 32, 128), F32),
            pltpu.VMEM((8, 128), F32),
            pltpu.VMEM((NPEER, 8, 128), F32),
            pltpu.VMEM((8, 128), F32),
            pltpu.VMEM((NZ, 8, 128), F32),
            pltpu.VMEM((8, 128), F32),
            pltpu.VMEM((8, 128), F32),
            dma((2, NPEER)), dma((2, NPEER)),
            dma((2, HALF + 1)), dma((2, HALF + 1)),
            dma((2, HALF + 1)), dma((2, HALF + 1)),
            dma((HALF,)), dma((HALF,)),
            dma((2, 2)), dma((2, 2)),
            dma((2, NPEER)), dma((2, NPEER)),
            dma((NPEER,)), dma((NPEER,)),
            dma((NZ,)), dma((NZ,)),
            dma, dma,
        ],
        compiler_params=pltpu.CompilerParams(
            collective_id=0, has_side_effects=True, vmem_limit_bytes=40 * 1024 * 1024
        ),
    )(points, lengthscale.reshape(1, 32), noise, direction, residual, solution)
    return (out[0], out[1], out[2], out[3].reshape(32))


def solution(mesh):
    data = P(None, ("wide", "narrow"))
    return jax.shard_map(
        body,
        mesh=mesh,
        in_specs=(data, P(), P(), data, data, data),
        out_specs=(data, data, data, P()),
        check_vma=False,
    )
```

```python
import functools
import math

import jax
import jax.numpy as jnp
from jax import lax
from jax.experimental import pallas as pl
from jax.experimental.pallas import tpu as pltpu
from jax.sharding import PartitionSpec as P

F32, BF16 = jnp.float32, jnp.bfloat16
MESH = pl.DeviceIdType.MESH
NX, NY, NZ = 4, 4, 16
NPEER = NX * NY
BLK = 192
CHUNK = NY * BLK
HOME = NPEER * BLK
VIS = 2 * BLK
HALF = NZ // 2
COORD_SCALE = math.sqrt(5.0) / 3.0
EXP_SCALE = -3.0 * math.log2(math.e)
EXP_SHIFT = math.log2(3.0)
NT = (((1,), (1,)), ((), ()))


def matern(u):
    u = jnp.maximum(u, 1e-30)
    q = u * lax.rsqrt(u)
    e = jnp.exp2(q * EXP_SCALE + EXP_SHIFT)
    return (((u + q) + (1.0 / 3.0)) * e).astype(BF16)


def pack_tail(tail):
    lane = lax.broadcasted_iota(jnp.int32, (16, 128), 1)
    return jnp.where(lane < 64, tail[0:16], pltpu.roll(tail[16:32], 64, 1))


def pack_high(tail):
    lane = lax.broadcasted_iota(jnp.int32, (16, 128), 1)
    return jnp.where(lane < 64, pltpu.roll(tail[0:16], 64, 1), tail[16:32])


def unpack_tails(a, b):
    lane = lax.broadcasted_iota(jnp.int32, (16, 128), 1)
    top = jnp.where(lane < 64, a, pltpu.roll(b, 64, 1))
    bottom = jnp.where(lane < 64, pltpu.roll(a, 64, 1), b)
    return jnp.concatenate([top, bottom], axis=0)


def unpack(blocks):
    heads = [b[0:32] for b in blocks]
    tails = [unpack_tails(blocks[i][32:48], blocks[i + 1][32:48]) for i in range(0, len(blocks), 2)]
    return jnp.concatenate(heads + tails, axis=1)


def split3(v):
    hi = v.astype(BF16)
    rest = v - hi.astype(F32)
    mid = rest.astype(BF16)
    lo = (rest - mid.astype(F32)).astype(BF16)
    return hi, mid, lo


def norm_rows(s, first):
    sq = jnp.sum(s * s, axis=0, keepdims=True)
    hi, mid, lo = (p.astype(F32) for p in split3(sq))
    row = lax.broadcasted_iota(jnp.int32, (16, s.shape[1]), 0)
    ones = jnp.where(row < 6, 1.0, 0.0)
    rows = jnp.where(row == first, hi, jnp.where(row == first + 1, mid, jnp.where(row == first + 2, lo, ones)))
    return rows.astype(BF16)


def home_operand(s):
    hi, mid, lo = split3(s)
    pad = jnp.zeros((48, s.shape[1]), BF16)
    return jnp.concatenate([hi, hi, mid, mid, hi, lo, norm_rows(s, 0), pad], axis=0)


def visitor_operand(s):
    hi, mid, lo = split3(s)
    hi, mid, lo = (p * BF16(-2.0) for p in (hi, mid, lo))
    pad = jnp.zeros((48, s.shape[1]), BF16)
    return jnp.concatenate([hi, mid, hi, mid, lo, hi, norm_rows(s, 3), pad], axis=0).T


def to_row(cols):
    lane = lax.broadcasted_iota(jnp.int32, (32, 128), 1)
    sub = lax.broadcasted_iota(jnp.int32, (32, 128), 0)
    out = jnp.zeros((32, 128), F32)
    for i, col in enumerate(cols):
        out = jnp.where(lane == sub + 32 * i, col, out)
    return jnp.sum(out, axis=0, keepdims=True)


def to_col(row, i):
    lane = lax.broadcasted_iota(jnp.int32, (32, 128), 1)
    sub = lax.broadcasted_iota(jnp.int32, (32, 128), 0)
    return jnp.sum(jnp.where(lane == sub + 32 * i, row, 0.0), axis=1, keepdims=True)


def kernel(
    pts_hbm, ls_hbm, noise_ref, dir_hbm, res_hbm,
    kd_out, coef_out,
    pts_ref, ls_ref, dir_ref, res_ref,
    tail, own_s, own_d, home_s, home_d, vis_s, vis_d, hb, hd, va, vd, hacc, ret, ret_tail, sum_head, sum_tail, red_tail,
    cross_a, cross_b, fin_a, fin_b, red_a, red_b, ar1_src, ar1, ar2_src, ar2, ar3_src, ar3,
    in_sem, home_send, home_recv, zs_send, z_recv, sib_send, sib_recv,
    cross_send, cross_recv, fin_send, fin_recv, red_send, red_recv, ar1_send, ar1_recv, ar2_send, ar2_recv, ar3_send, ar3_recv,
):
    wide, narrow = lax.axis_index("wide"), lax.axis_index("narrow")
    z, y_hi, core = wide // 4, (wide // 2) % 2, wide % 2
    x, y_lo = narrow // 2, narrow % 2
    y = y_hi * 2 + y_lo

    def peer(dz=0, dx=0, dy=0, dc=0):
        pz, px, py, pc = (z + dz) % NZ, (x + dx) % NX, (y + dy) % NY, (core + dc) % 2
        return (pz * 4 + (py // 2) * 2 + pc, px * 2 + py % 2)

    def remote(src, dst, send, recv, dev):
        return pltpu.make_async_remote_copy(
            src_ref=src, dst_ref=dst, send_sem=send, recv_sem=recv, device_id=dev, device_id_type=MESH
        )

    plane = [(dx, dy) for dx in range(NX) for dy in range(NY)]

    fetches = [
        pltpu.make_async_copy(src, dst, in_sem.at[i])
        for i, (src, dst) in enumerate(((pts_hbm, pts_ref), (ls_hbm, ls_ref), (dir_hbm, dir_ref), (res_hbm, res_ref)))
    ]
    for fetch in fetches:
        fetch.start()

    barrier = pltpu.get_barrier_semaphore()
    senders = [dict(dx=dx, dy=dy) for dx, dy in plane[1:]] + [dict(dz=1), dict(dz=2), dict(dc=1)]
    for sender in senders:
        pl.semaphore_signal(barrier, inc=1, device_id=peer(**sender), device_id_type=MESH)

    for fetch in fetches[:3]:
        fetch.wait()
    eye = lax.broadcasted_iota(jnp.int32, (32, 32), 0) == lax.broadcasted_iota(jnp.int32, (32, 32), 1)
    scale = jnp.sum(jnp.where(eye, ls_ref[...], 0.0), axis=1, keepdims=True)
    scaled = pts_ref[...] / scale * COORD_SCALE
    own_s[0:32] = scaled[:, 0:128]
    tail[...] = jnp.zeros_like(tail)
    tail[:, 0:64] = scaled[:, 128:192]
    own_s[32:48] = pack_tail(tail[...])
    own_d[0:32] = dir_ref[:, 0:128].astype(BF16)
    tail[:, 0:64] = dir_ref[:, 128:192]
    own_d[32:48] = pack_tail(tail[...]).astype(BF16)

    hacc[...] = jnp.zeros_like(hacc)
    ret[...] = jnp.zeros_like(ret)
    pl.semaphore_wait(barrier, len(senders))

    own, vis, home = (own_s, own_d), (vis_s, vis_d), (home_s, home_d)

    def home_copy(dx, dy, slot, which):
        return remote(
            own[which], home[which].at[slot], home_send.at[which, dx * NY + dy], home_recv.at[which, slot], peer(dx=dx, dy=dy)
        )

    def z_copy(k, which):
        src = own[which] if k <= 2 else vis[which].at[k - 2, 0]
        return remote(src, vis[which].at[k, 0], zs_send.at[which, k], z_recv.at[which, k], peer(dz=NZ - min(k, 2)))

    def sib_copy(k, which):
        src = own[which] if k == 0 else vis[which].at[k, 0]
        return remote(src, vis[which].at[k, 1], sib_send.at[which, k], sib_recv.at[which, k], peer(dc=1))

    def home_start(which):
        for dx, dy in plane[1:]:
            home_copy(dx, dy, ((-dx) % NX) * NY + (-dy) % NY, which).start()

    for which in range(2):
        sib_copy(0, which).start()
    for k in (1, 2):
        for which in range(2):
            z_copy(k, which).start()
    home_start(0)
    home_start(1)

    vis_s[0, 0] = own_s[...]
    vis_d[0, 0] = own_d[...]
    home_s[0] = own_s[...]
    home_d[0] = own_d[...]

    def set_visitors(k, at):
        va[at:at + VIS] = visitor_operand(unpack([vis_s[k, 0], vis_s[k, 1]]))
        vd[:, at:at + VIS] = unpack([vis_d[k, 0].astype(F32), vis_d[k, 1].astype(F32)]).astype(BF16)

    def pass_on(k):
        for which in range(2):
            z_copy(k, which).wait_recv()
        for which in range(2):
            sib_copy(k, which).start()
            if k + 2 <= HALF:
                z_copy(k + 2, which).start()

    def columns(g):
        return pl.ds(pl.multiple_of(g * CHUNK, CHUNK), CHUNK)

    for which in range(2):
        sib_copy(0, which).wait_recv()
    set_visitors(0, 0)

    def first(g, carry):
        for dy in range(NY):
            copy = home_copy(g, dy, g * NY + dy, 0)
            if dy:
                copy.wait_recv()
            else:
                pl.when(g > 0)(copy.wait_recv)
        cols = columns(g)
        hb[:, cols] = home_operand(unpack([home_s[g * NY + dy] for dy in range(NY)]))
        tile = matern(jnp.dot(va[0:VIS], hb[:, cols], preferred_element_type=F32))
        hacc[:, cols] += jnp.dot(vd[:, 0:VIS], tile, preferred_element_type=F32)

        @pl.when(g == 1)
        def _():
            pass_on(1)
            pass_on(2)

        return carry

    lax.fori_loop(0, NX, first, 0)
    for dx, dy in plane[1:]:
        home_copy(dx, dy, dx * NY + dy, 1).wait_recv()
    for g in range(NX):
        hd[:, columns(g)] = unpack([home_d[g * NY + dy].astype(F32) for dy in range(NY)]).astype(BF16)

    def cross_copy(k, part):
        pair, half = (k - 1) // 2, (k - 1) % 2
        src = ret.at[pair, :, pl.ds(VIS * half + 128, 128)] if part == 0 else ret_tail.at[k]
        dst = (cross_a, cross_b)[part].at[k]
        return remote(src, dst, cross_send.at[k, part], cross_recv.at[k, part], peer(dc=1))

    def fin_copy(k, part):
        src, dst = ((sum_head, fin_a), (sum_tail, fin_b))[part]
        return remote(src.at[k], dst.at[k], fin_send.at[k, part], fin_recv.at[k, part], peer(dz=k))

    def exchange(ks):
        for k in ks:
            pair, half = (k - 1) // 2, (k - 1) % 2
            ret_tail[k] = pack_high(ret[pair, :, pl.ds(VIS * half + 256, 128)])
            for part in range(2):
                cross_copy(k, part).start()

    def send_home(ks):
        for k in ks:
            pair, half = (k - 1) // 2, (k - 1) % 2
            for part in range(2):
                cross_copy(k, part).wait_recv()
            sum_head[k] = ret[pair, :, pl.ds(VIS * half, 128)] + cross_a[k]
            sum_tail[k] = pack_tail(ret[pair, :, pl.ds(VIS * half + 256, 128)]) + cross_b[k]
            for part in range(2):
                fin_copy(k, part).start()

    def visitors(k, at):
        for which in range(2):
            sib_copy(k, which).wait_recv()
        set_visitors(k, at)

    for pair in range(3):
        pass_on(2 * pair + 3)
        pass_on(2 * pair + 4)
        visitors(2 * pair + 1, 0)
        visitors(2 * pair + 2, VIS)

        def both(g, carry, pair=pair):
            cols = columns(g)
            tile = matern(jnp.dot(va[...], hb[:, cols], preferred_element_type=F32))
            hacc[:, cols] += jnp.dot(vd[...], tile, preferred_element_type=F32)
            ret[pair] += lax.dot_general(hd[:, cols], tile, NT, preferred_element_type=F32)
            if pair:
                pl.when(g == 1)(functools.partial(send_home, (2 * pair - 1, 2 * pair)))
            return carry

        lax.fori_loop(0, NX, both, 0)
        exchange((2 * pair + 1, 2 * pair + 2))

    visitors(7, 0)
    visitors(8, VIS)

    def seventh(g, carry):
        cols = columns(g)
        tile = matern(jnp.dot(va[0:VIS], hb[:, cols], preferred_element_type=F32))
        hacc[:, cols] += jnp.dot(vd[:, 0:VIS], tile, preferred_element_type=F32)
        ret[3, :, 0:VIS] += lax.dot_general(hd[:, cols], tile, NT, preferred_element_type=F32)
        pl.when(g == 1)(functools.partial(send_home, (5, 6)))
        return carry

    lax.fori_loop(0, NX, seventh, 0)
    exchange((7,))

    def red_copy(dx, dy, slot, part):
        base = dx * CHUNK + 128 * dy
        src = hacc.at[:, pl.ds(pl.multiple_of(base, 128), 128)] if part == 0 else red_tail.at[dx * NY + dy]
        dst = (red_a, red_b)[part].at[slot]
        return remote(src, dst, red_send.at[part, dx * NY + dy], red_recv.at[part, slot], peer(dx=dx, dy=dy))

    def back(dx, dy):
        return ((NX - dx) % NX) * NY + (NY - dy) % NY

    def eighth(t, carry):
        g = (t + 1) % NX
        cols = columns(g)
        tile = matern(jnp.dot(va[VIS:2 * VIS], hb[:, cols], preferred_element_type=F32))
        hacc[:, cols] += jnp.dot(vd[:, VIS:2 * VIS], tile, preferred_element_type=F32)
        for dy in range(NY):
            tails = hacc[:, pl.ds(pl.multiple_of(g * CHUNK + 512 + 128 * (dy // 2), 128), 128)]
            red_tail[g * NY + dy] = pack_high(tails) if dy % 2 else pack_tail(tails)

        def send(dy):
            for part in range(2):
                red_copy(g, dy, back(g, dy), part).start()

        for dy in range(1, NY):
            send(dy)
        pl.when(g > 0)(functools.partial(send, 0))
        pl.when(t == 1)(functools.partial(send_home, (7,)))
        return carry

    lax.fori_loop(0, NX, eighth, 0)

    fetches[3].wait()
    direction = dir_ref[...]
    residual = res_ref[...]
    sum_a, sum_b = hacc[:, 0:128], red_tail[0]
    for dx, dy in plane[1:]:
        for part in range(2):
            red_copy(dx, dy, dx * NY + dy, part).wait_recv()
        sum_a = sum_a + red_a[dx * NY + dy]
        sum_b = sum_b + red_b[dx * NY + dy]
    for k in range(1, HALF):
        for part in range(2):
            fin_copy(k, part).wait_recv()
        sum_a = sum_a + fin_a[k]
        sum_b = sum_b + fin_b[k]
    last_points = jnp.concatenate([sum_b, pltpu.roll(sum_b, 64, 1)], axis=0)[:, 0:64]
    kd = jnp.concatenate([sum_a, last_points], axis=1) + noise_ref[0] * direction
    kd_out[...] = kd

    def total(v):
        return jnp.sum(v, axis=1, keepdims=True)

    sums = to_row([total(residual * residual), total(direction * kd), total(residual * kd), total(kd * kd)])

    ar1_src[...] = jnp.broadcast_to(sums, (8, 128))
    me1 = x * NY + y

    def ar1_copy(dx, dy, slot):
        return remote(ar1_src, ar1.at[slot], ar1_send.at[dx * NY + dy], ar1_recv.at[slot], peer(dx=dx, dy=dy))

    for dx, dy in plane[1:]:
        ar1_copy(dx, dy, me1).start()
    ar1[me1] = ar1_src[...]
    for dx, dy in plane[1:]:
        ar1_copy(dx, dy, ((x + dx) % NX) * NY + (y + dy) % NY).wait_recv()
    acc = ar1[0]
    for i in range(1, NPEER):
        acc = acc + ar1[i]
    ar2_src[...] = acc

    def ar2_copy(dz, slot):
        return remote(ar2_src, ar2.at[slot], ar2_send.at[dz], ar2_recv.at[slot], peer(dz=dz))

    for dz in range(1, NZ):
        ar2_copy(dz, z).start()
    ar2[z] = acc
    for dz in range(1, NZ):
        ar2_copy(dz, (z + dz) % NZ).wait_recv()
    acc = ar2[0]
    for i in range(1, NZ):
        acc = acc + ar2[i]
    ar3_src[...] = acc
    last = remote(ar3_src, ar3, ar3_send, ar3_recv, peer(dc=1))
    last.start()
    last.wait_recv()
    acc = (ar3_src[...] + ar3[...])[0:1]

    rr, curve, r_kd, kd_sq = (to_col(acc, i) for i in range(4))
    alpha = rr / curve
    norm_sq = rr - 2.0 * alpha * r_kd + alpha * alpha * kd_sq
    lane = lax.broadcasted_iota(jnp.int32, (32, 128), 1)
    coef_out[...] = jnp.where(lane == 0, alpha, jnp.where(lane == 1, norm_sq / rr, norm_sq))

    for which in range(2):
        for pos in range(HALF + 1):
            if pos:
                z_copy(pos, which).wait_send()
            sib_copy(pos, which).wait_send()
        for dx, dy in plane[1:]:
            home_copy(dx, dy, dx * NY + dy, which).wait_send()
            red_copy(dx, dy, dx * NY + dy, which).wait_send()
    for k in range(1, HALF):
        for part in range(2):
            cross_copy(k, part).wait_send()
            fin_copy(k, part).wait_send()
    for dx, dy in plane[1:]:
        ar1_copy(dx, dy, me1).wait_send()
    for dz in range(1, NZ):
        ar2_copy(dz, z).wait_send()
    last.wait_send()


def body(points, lengthscale, noise, direction, residual, solution):
    vmem, smem = pl.BlockSpec(memory_space=pltpu.VMEM), pl.BlockSpec(memory_space=pltpu.SMEM)
    hbm = pl.BlockSpec(memory_space=pl.ANY)
    dma = pltpu.SemaphoreType.DMA
    kd, coef = pl.pallas_call(
        kernel,
        out_shape=[jax.ShapeDtypeStruct((32, BLK), F32), jax.ShapeDtypeStruct((32, 128), F32)],
        in_specs=[hbm, hbm, smem, hbm, hbm],
        out_specs=[vmem] * 2,
        scratch_shapes=[
            pltpu.VMEM((32, BLK), F32),
            pltpu.VMEM((1, 32), F32),
            pltpu.VMEM((32, BLK), F32),
            pltpu.VMEM((32, BLK), F32),
            pltpu.VMEM((32, 128), F32),
            pltpu.VMEM((48, 128), F32),
            pltpu.VMEM((48, 128), BF16),
            pltpu.VMEM((NPEER, 48, 128), F32),
            pltpu.VMEM((NPEER, 48, 128), BF16),
            pltpu.VMEM((HALF + 1, 2, 48, 128), F32),
            pltpu.VMEM((HALF + 1, 2, 48, 128), BF16),
            pltpu.VMEM((256, HOME), BF16),
            pltpu.VMEM((32, HOME), BF16),
            pltpu.VMEM((2 * VIS, 256), BF16),
            pltpu.VMEM((32, 2 * VIS), BF16),
            pltpu.VMEM((32, HOME), F32),
            pltpu.VMEM((HALF // 2, 32, 2 * VIS), F32),
            pltpu.VMEM((HALF, 16, 128), F32),
            pltpu.VMEM((HALF, 32, 128), F32),
            pltpu.VMEM((HALF, 16, 128), F32),
            pltpu.VMEM((NPEER, 16, 128), F32),
            pltpu.VMEM((HALF, 32, 128), F32),
            pltpu.VMEM((HALF, 16, 128), F32),
            pltpu.VMEM((HALF, 32, 128), F32),
            pltpu.VMEM((HALF, 16, 128), F32),
            pltpu.VMEM((NPEER, 32, 128), F32),
            pltpu.VMEM((NPEER, 16, 128), F32),
            pltpu.VMEM((8, 128), F32),
            pltpu.VMEM((NPEER, 8, 128), F32),
            pltpu.VMEM((8, 128), F32),
            pltpu.VMEM((NZ, 8, 128), F32),
            pltpu.VMEM((8, 128), F32),
            pltpu.VMEM((8, 128), F32),
            dma((4,)),
            dma((2, NPEER)), dma((2, NPEER)),
            dma((2, HALF + 1)), dma((2, HALF + 1)),
            dma((2, HALF + 1)), dma((2, HALF + 1)),
            dma((HALF, 2)), dma((HALF, 2)),
            dma((HALF, 2)), dma((HALF, 2)),
            dma((2, NPEER)), dma((2, NPEER)),
            dma((NPEER,)), dma((NPEER,)),
            dma((NZ,)), dma((NZ,)),
            dma, dma,
        ],
        compiler_params=pltpu.CompilerParams(
            collective_id=0, has_side_effects=True, vmem_limit_bytes=63 * 1024 * 1024
        ),
    )(points, lengthscale.reshape(1, 32), noise, direction, residual)
    alpha, beta = coef[:, 0:1], coef[:, 1:2]
    new_residual = residual - alpha * kd
    return (solution + alpha * direction, new_residual, new_residual + beta * direction, coef[:, 2])


def solution(mesh):
    data = P(None, ("wide", "narrow"))
    return jax.shard_map(
        body,
        mesh=mesh,
        in_specs=(data, P(), P(), data, data, data),
        out_specs=(data, data, data, P()),
        check_vma=False,
    )
```

```python
import functools
import math

import jax
import jax.numpy as jnp
from jax import lax
from jax.experimental import pallas as pl
from jax.experimental.pallas import tpu as pltpu
from jax.sharding import PartitionSpec as P

F32, BF16 = jnp.float32, jnp.bfloat16
MESH = pl.DeviceIdType.MESH
NX, NY, NZ = 4, 4, 16
NPEER = NX * NY
BLK = 192
CHUNK = NY * BLK
HOME = NPEER * BLK
VIS = 2 * BLK
HALF = NZ // 2
COORD_SCALE = math.sqrt(5.0) / 3.0
EXP_SCALE = -3.0 * math.log2(math.e)
EXP_SHIFT = math.log2(3.0)
NT = (((1,), (1,)), ((), ()))


def matern(u):
    u = jnp.maximum(u, 1e-30)
    q = u * lax.rsqrt(u)
    e = jnp.exp2(q * EXP_SCALE + EXP_SHIFT)
    return (((u + q) + (1.0 / 3.0)) * e).astype(BF16)


def pack_tail(tail):
    lane = lax.broadcasted_iota(jnp.int32, (16, 128), 1)
    return jnp.where(lane < 64, tail[0:16], pltpu.roll(tail[16:32], 64, 1))


def pack_high(tail):
    lane = lax.broadcasted_iota(jnp.int32, (16, 128), 1)
    return jnp.where(lane < 64, pltpu.roll(tail[0:16], 64, 1), tail[16:32])


def unpack_tails(a, b):
    lane = lax.broadcasted_iota(jnp.int32, (16, 128), 1)
    top = jnp.where(lane < 64, a, pltpu.roll(b, 64, 1))
    bottom = jnp.where(lane < 64, pltpu.roll(a, 64, 1), b)
    return jnp.concatenate([top, bottom], axis=0)


def unpack(blocks):
    heads = [b[0:32] for b in blocks]
    tails = [unpack_tails(blocks[i][32:48], blocks[i + 1][32:48]) for i in range(0, len(blocks), 2)]
    return jnp.concatenate(heads + tails, axis=1)


def split3(v):
    hi = v.astype(BF16)
    rest = v - hi.astype(F32)
    mid = rest.astype(BF16)
    lo = (rest - mid.astype(F32)).astype(BF16)
    return hi, mid, lo


def norm_rows(s, first):
    sq = jnp.sum(s * s, axis=0, keepdims=True)
    hi, mid, lo = (p.astype(F32) for p in split3(sq))
    row = lax.broadcasted_iota(jnp.int32, (16, s.shape[1]), 0)
    ones = jnp.where(row < 6, 1.0, 0.0)
    rows = jnp.where(row == first, hi, jnp.where(row == first + 1, mid, jnp.where(row == first + 2, lo, ones)))
    return rows.astype(BF16)


def home_operand(s):
    hi, mid, lo = split3(s)
    pad = jnp.zeros((48, s.shape[1]), BF16)
    return jnp.concatenate([hi, hi, mid, mid, hi, lo, norm_rows(s, 0), pad], axis=0)


def visitor_operand(s):
    hi, mid, lo = split3(s)
    hi, mid, lo = (p * BF16(-2.0) for p in (hi, mid, lo))
    pad = jnp.zeros((48, s.shape[1]), BF16)
    return jnp.concatenate([hi, mid, hi, mid, lo, hi, norm_rows(s, 3), pad], axis=0).T


def to_row(cols):
    lane = lax.broadcasted_iota(jnp.int32, (32, 128), 1)
    sub = lax.broadcasted_iota(jnp.int32, (32, 128), 0)
    out = jnp.zeros((32, 128), F32)
    for i, col in enumerate(cols):
        out = jnp.where(lane == sub + 32 * i, col, out)
    return jnp.sum(out, axis=0, keepdims=True)


def to_col(row, i):
    lane = lax.broadcasted_iota(jnp.int32, (32, 128), 1)
    sub = lax.broadcasted_iota(jnp.int32, (32, 128), 0)
    return jnp.sum(jnp.where(lane == sub + 32 * i, row, 0.0), axis=1, keepdims=True)


def kernel(
    pts_hbm, ls_hbm, noise_ref, dir_hbm, res_hbm,
    kd_out, alpha_out, beta_out, norm_out,
    pts_ref, ls_ref, dir_ref, res_ref,
    tail, own_s, own_d, home_s, home_d, vis_s, vis_d, hb, hd, va, vd, hacc, ret, ret_tail, sum_head, sum_tail, red_tail,
    cross_a, cross_b, fin_a, fin_b, red_a, red_b, ar1_src, ar1, ar2_src, ar2,
    in_sem, home_send, home_recv, zs_send, z_recv, sib_send, sib_recv,
    cross_send, cross_recv, fin_send, fin_recv, red_send, red_recv, ar1_send, ar1_recv, ar2_send, ar2_recv,
):
    wide, narrow = lax.axis_index("wide"), lax.axis_index("narrow")
    z, y_hi, core = wide // 4, (wide // 2) % 2, wide % 2
    x, y_lo = narrow // 2, narrow % 2
    y = y_hi * 2 + y_lo

    def peer(dz=0, dx=0, dy=0, dc=0):
        pz, px, py, pc = (z + dz) % NZ, (x + dx) % NX, (y + dy) % NY, (core + dc) % 2
        return (pz * 4 + (py // 2) * 2 + pc, px * 2 + py % 2)

    def remote(src, dst, send, recv, dev):
        return pltpu.make_async_remote_copy(
            src_ref=src, dst_ref=dst, send_sem=send, recv_sem=recv, device_id=dev, device_id_type=MESH
        )

    plane = [(dx, dy) for dx in range(NX) for dy in range(NY)]

    fetches = [
        pltpu.make_async_copy(src, dst, in_sem.at[i])
        for i, (src, dst) in enumerate(((pts_hbm, pts_ref), (ls_hbm, ls_ref), (dir_hbm, dir_ref), (res_hbm, res_ref)))
    ]
    for fetch in fetches:
        fetch.start()

    barrier = pltpu.get_barrier_semaphore()
    senders = [dict(dx=dx, dy=dy) for dx, dy in plane[1:]] + [dict(dz=1), dict(dz=2), dict(dc=1)]
    for sender in senders:
        pl.semaphore_signal(barrier, inc=1, device_id=peer(**sender), device_id_type=MESH)

    for fetch in fetches[:3]:
        fetch.wait()
    eye = lax.broadcasted_iota(jnp.int32, (32, 32), 0) == lax.broadcasted_iota(jnp.int32, (32, 32), 1)
    scale = jnp.sum(jnp.where(eye, ls_ref[...], 0.0), axis=1, keepdims=True)
    scaled = pts_ref[...] / scale * COORD_SCALE
    own_s[0:32] = scaled[:, 0:128]
    tail[...] = jnp.zeros_like(tail)
    tail[:, 0:64] = scaled[:, 128:192]
    own_s[32:48] = pack_tail(tail[...])
    own_d[0:32] = dir_ref[:, 0:128].astype(BF16)
    tail[:, 0:64] = dir_ref[:, 128:192]
    own_d[32:48] = pack_tail(tail[...]).astype(BF16)

    hacc[...] = jnp.zeros_like(hacc)
    ret[...] = jnp.zeros_like(ret)
    pl.semaphore_wait(barrier, len(senders))

    own, vis, home = (own_s, own_d), (vis_s, vis_d), (home_s, home_d)

    def home_copy(dx, dy, slot, which):
        return remote(
            own[which], home[which].at[slot], home_send.at[which, dx * NY + dy], home_recv.at[which, slot], peer(dx=dx, dy=dy)
        )

    def z_copy(k, which):
        src = own[which] if k <= 2 else vis[which].at[k - 2, 0]
        return remote(src, vis[which].at[k, 0], zs_send.at[which, k], z_recv.at[which, k], peer(dz=NZ - min(k, 2)))

    def sib_copy(k, which):
        src = own[which] if k == 0 else vis[which].at[k, 0]
        return remote(src, vis[which].at[k, 1], sib_send.at[which, k], sib_recv.at[which, k], peer(dc=1))

    for which in range(2):
        sib_copy(0, which).start()
    for k in (1, 2):
        for which in range(2):
            z_copy(k, which).start()
    for dx in (0, 1, 3, 2):
        for dy in range(NY):
            if dx or dy:
                for which in range(2):
                    home_copy(dx, dy, ((-dx) % NX) * NY + (-dy) % NY, which).start()

    vis_s[0, 0] = own_s[...]
    vis_d[0, 0] = own_d[...]
    home_s[0] = own_s[...]
    home_d[0] = own_d[...]

    def set_visitors(k, at):
        va[at:at + VIS] = visitor_operand(unpack([vis_s[k, 0], vis_s[k, 1]]))
        vd[:, at:at + VIS] = unpack([vis_d[k, 0].astype(F32), vis_d[k, 1].astype(F32)]).astype(BF16)

    def pass_on(k):
        for which in range(2):
            z_copy(k, which).wait_recv()
        for which in range(2):
            sib_copy(k, which).start()
            if k + 2 <= HALF:
                z_copy(k + 2, which).start()

    def columns(g):
        return pl.ds(pl.multiple_of(g * CHUNK, CHUNK), CHUNK)

    def visitors(k, at):
        for which in range(2):
            sib_copy(k, which).wait_recv()
        set_visitors(k, at)

    def begin():
        for k in (1, 2):
            pass_on(k)
        for k in (1, 2):
            visitors(k, VIS * (k - 1))

    def first(t, carry):
        g = t + (t // 2) * (5 - 2 * t)
        for dy in range(NY):
            for which in range(2):
                copy = home_copy(g, dy, g * NY + dy, which)
                if dy:
                    copy.wait_recv()
                else:
                    pl.when(t > 0)(copy.wait_recv)
        cols = columns(g)
        hb[:, cols] = home_operand(unpack([home_s[g * NY + dy] for dy in range(NY)]))
        hd[:, cols] = unpack([home_d[g * NY + dy].astype(F32) for dy in range(NY)]).astype(BF16)
        pl.when(t == 0)(begin)

        @pl.when(t == 2)
        def _():
            pass_on(3)
            pass_on(4)

        tile = matern(jnp.dot(va[...], hb[:, cols], preferred_element_type=F32))
        hacc[:, cols] += jnp.dot(vd[...], tile, preferred_element_type=F32)
        ret[0] += lax.dot_general(hd[:, cols], tile, NT, preferred_element_type=F32)
        return carry

    lax.fori_loop(0, NX, first, 0)

    def cross_copy(k, part):
        pair, half = (k - 1) // 2, (k - 1) % 2
        src = ret.at[pair, :, pl.ds(VIS * half + 128, 128)] if part == 0 else ret_tail.at[k]
        dst = (cross_a, cross_b)[part].at[k]
        return remote(src, dst, cross_send.at[k, part], cross_recv.at[k, part], peer(dc=1))

    def fin_copy(k, part):
        src, dst = ((sum_head, fin_a), (sum_tail, fin_b))[part]
        return remote(src.at[k], dst.at[k], fin_send.at[k, part], fin_recv.at[k, part], peer(dz=k))

    def exchange(ks):
        for k in ks:
            pair, half = (k - 1) // 2, (k - 1) % 2
            ret_tail[k] = pack_high(ret[pair, :, pl.ds(VIS * half + 256, 128)])
            for part in range(2):
                cross_copy(k, part).start()

    def send_home(ks):
        for k in ks:
            pair, half = (k - 1) // 2, (k - 1) % 2
            for part in range(2):
                cross_copy(k, part).wait_recv()
            sum_head[k] = ret[pair, :, pl.ds(VIS * half, 128)] + cross_a[k]
            sum_tail[k] = pack_tail(ret[pair, :, pl.ds(VIS * half + 256, 128)]) + cross_b[k]
            for part in range(2):
                fin_copy(k, part).start()

    exchange((1, 2))

    for pair in (1, 2):
        visitors(2 * pair + 1, 0)
        visitors(2 * pair + 2, VIS)

        def both(g, carry, pair=pair):
            cols = columns(g)
            tile = matern(jnp.dot(va[...], hb[:, cols], preferred_element_type=F32))
            hacc[:, cols] += jnp.dot(vd[...], tile, preferred_element_type=F32)
            ret[pair] += lax.dot_general(hd[:, cols], tile, NT, preferred_element_type=F32)

            @pl.when(g == 1)
            def _():
                pass_on(2 * pair + 3)
                pass_on(2 * pair + 4)
                send_home((2 * pair - 1, 2 * pair))

            return carry

        lax.fori_loop(0, NX, both, 0)
        exchange((2 * pair + 1, 2 * pair + 2))

    visitors(7, 0)

    def seventh(g, carry):
        cols = columns(g)
        tile = matern(jnp.dot(va[0:VIS], hb[:, cols], preferred_element_type=F32))
        hacc[:, cols] += jnp.dot(vd[:, 0:VIS], tile, preferred_element_type=F32)
        ret[3, :, 0:VIS] += lax.dot_general(hd[:, cols], tile, NT, preferred_element_type=F32)
        pl.when(g == 1)(functools.partial(send_home, (5, 6)))
        return carry

    lax.fori_loop(0, NX, seventh, 0)
    exchange((7,))

    visitors(8, 0)
    visitors(0, VIS)
    def red_copy(dx, dy, slot, part):
        base = dx * CHUNK + 128 * dy
        src = hacc.at[:, pl.ds(pl.multiple_of(base, 128), 128)] if part == 0 else red_tail.at[dx * NY + dy]
        dst = (red_a, red_b)[part].at[slot]
        return remote(src, dst, red_send.at[part, dx * NY + dy], red_recv.at[part, slot], peer(dx=dx, dy=dy))

    def back(dx, dy):
        return ((NX - dx) % NX) * NY + (NY - dy) % NY

    def last_pair(t, carry):
        g = (t + 1) % NX
        cols = columns(g)
        tile = matern(jnp.dot(va[...], hb[:, cols], preferred_element_type=F32))
        hacc[:, cols] += jnp.dot(vd[...], tile, preferred_element_type=F32)
        for dy in range(NY):
            tails = hacc[:, pl.ds(pl.multiple_of(g * CHUNK + 512 + 128 * (dy // 2), 128), 128)]
            red_tail[g * NY + dy] = pack_high(tails) if dy % 2 else pack_tail(tails)

        def send(dy):
            for part in range(2):
                red_copy(g, dy, back(g, dy), part).start()

        for dy in range(1, NY):
            send(dy)
        pl.when(g > 0)(functools.partial(send, 0))
        pl.when(t == 0)(functools.partial(send_home, (7,)))
        return carry

    lax.fori_loop(0, NX, last_pair, 0)

    fetches[3].wait()
    direction = dir_ref[...]
    residual = res_ref[...]
    sum_a, sum_b = hacc[:, 0:128], red_tail[0]
    for dx, dy in plane[1:]:
        for part in range(2):
            red_copy(dx, dy, dx * NY + dy, part).wait_recv()
        sum_a = sum_a + red_a[dx * NY + dy]
        sum_b = sum_b + red_b[dx * NY + dy]
    for k in range(1, HALF):
        for part in range(2):
            fin_copy(k, part).wait_recv()
        sum_a = sum_a + fin_a[k]
        sum_b = sum_b + fin_b[k]
    last_points = jnp.concatenate([sum_b, pltpu.roll(sum_b, 64, 1)], axis=0)[:, 0:64]
    kd = jnp.concatenate([sum_a, last_points], axis=1) + noise_ref[0] * direction
    kd_out[...] = kd

    def total(v):
        return jnp.sum(v, axis=1, keepdims=True)

    sums = to_row([total(residual * residual), total(direction * kd), total(residual * kd), total(kd * kd)])

    ar1_src[...] = sums
    me1 = (x * NY + y) * 2 + core
    near = [(dx, dy, dc) for dx, dy in plane for dc in range(2)][1:]

    def ar1_copy(dx, dy, dc, slot):
        i = (dx * NY + dy) * 2 + dc
        return remote(ar1_src, ar1.at[slot], ar1_send.at[i], ar1_recv.at[slot], peer(dx=dx, dy=dy, dc=dc))

    for dx, dy, dc in near:
        ar1_copy(dx, dy, dc, me1).start()
    ar1[me1] = sums
    for which in range(2):
        for pos in range(HALF + 1):
            if pos:
                z_copy(pos, which).wait_send()
            sib_copy(pos, which).wait_send()
        for dx, dy in plane[1:]:
            home_copy(dx, dy, dx * NY + dy, which).wait_send()
            red_copy(dx, dy, dx * NY + dy, which).wait_send()
    for k in range(1, HALF):
        for part in range(2):
            cross_copy(k, part).wait_send()
            fin_copy(k, part).wait_send()
    for dx, dy, dc in near:
        ar1_copy(dx, dy, dc, (((x + dx) % NX) * NY + (y + dy) % NY) * 2 + (core + dc) % 2).wait_recv()
    acc = jnp.sum(ar1[...], axis=0)
    ar2_src[...] = acc

    def ar2_copy(dz, slot):
        return remote(ar2_src, ar2.at[slot], ar2_send.at[dz], ar2_recv.at[slot], peer(dz=dz))

    for dz in range(1, NZ):
        ar2_copy(dz, z).start()
    ar2[z] = acc
    for dz in range(1, NZ):
        ar2_copy(dz, (z + dz) % NZ).wait_recv()
    acc = jnp.sum(ar2[...], axis=0)

    rr, curve, r_kd, kd_sq = (to_col(acc, i) for i in range(4))
    alpha = rr / curve
    norm_sq = rr - 2.0 * alpha * r_kd + alpha * alpha * kd_sq
    alpha_out[...] = jnp.broadcast_to(alpha, (32, BLK))
    beta_out[...] = jnp.broadcast_to(norm_sq / rr, (32, BLK))
    norm_out[...] = jnp.sum(jnp.where(eye, norm_sq, 0.0), axis=0, keepdims=True)

    for dx, dy, dc in near:
        ar1_copy(dx, dy, dc, me1).wait_send()
    for dz in range(1, NZ):
        ar2_copy(dz, z).wait_send()


def body(points, lengthscale, noise, direction, residual, solution):
    vmem, smem = pl.BlockSpec(memory_space=pltpu.VMEM), pl.BlockSpec(memory_space=pltpu.SMEM)
    hbm = pl.BlockSpec(memory_space=pl.ANY)
    dma = pltpu.SemaphoreType.DMA
    block = jax.ShapeDtypeStruct((32, BLK), F32)
    kd, alpha, beta, norm_sq = pl.pallas_call(
        kernel,
        out_shape=[block, block, block, jax.ShapeDtypeStruct((1, 32), F32)],
        in_specs=[hbm, hbm, smem, hbm, hbm],
        out_specs=[vmem] * 4,
        scratch_shapes=[
            pltpu.VMEM((32, BLK), F32),
            pltpu.VMEM((1, 32), F32),
            pltpu.VMEM((32, BLK), F32),
            pltpu.VMEM((32, BLK), F32),
            pltpu.VMEM((32, 128), F32),
            pltpu.VMEM((48, 128), F32),
            pltpu.VMEM((48, 128), BF16),
            pltpu.VMEM((NPEER, 48, 128), F32),
            pltpu.VMEM((NPEER, 48, 128), BF16),
            pltpu.VMEM((HALF + 1, 2, 48, 128), F32),
            pltpu.VMEM((HALF + 1, 2, 48, 128), BF16),
            pltpu.VMEM((256, HOME), BF16),
            pltpu.VMEM((32, HOME), BF16),
            pltpu.VMEM((2 * VIS, 256), BF16),
            pltpu.VMEM((32, 2 * VIS), BF16),
            pltpu.VMEM((32, HOME), F32),
            pltpu.VMEM((HALF // 2, 32, 2 * VIS), F32),
            pltpu.VMEM((HALF, 16, 128), F32),
            pltpu.VMEM((HALF, 32, 128), F32),
            pltpu.VMEM((HALF, 16, 128), F32),
            pltpu.VMEM((NPEER, 16, 128), F32),
            pltpu.VMEM((HALF, 32, 128), F32),
            pltpu.VMEM((HALF, 16, 128), F32),
            pltpu.VMEM((HALF, 32, 128), F32),
            pltpu.VMEM((HALF, 16, 128), F32),
            pltpu.VMEM((NPEER, 32, 128), F32),
            pltpu.VMEM((NPEER, 16, 128), F32),
            pltpu.VMEM((1, 128), F32),
            pltpu.VMEM((2 * NPEER, 1, 128), F32),
            pltpu.VMEM((1, 128), F32),
            pltpu.VMEM((NZ, 1, 128), F32),
            dma((4,)),
            dma((2, NPEER)), dma((2, NPEER)),
            dma((2, HALF + 1)), dma((2, HALF + 1)),
            dma((2, HALF + 1)), dma((2, HALF + 1)),
            dma((HALF, 2)), dma((HALF, 2)),
            dma((HALF, 2)), dma((HALF, 2)),
            dma((2, NPEER)), dma((2, NPEER)),
            dma((2 * NPEER,)), dma((2 * NPEER,)),
            dma((NZ,)), dma((NZ,)),
        ],
        compiler_params=pltpu.CompilerParams(
            collective_id=0, has_side_effects=True, vmem_limit_bytes=63 * 1024 * 1024
        ),
    )(points, lengthscale.reshape(1, 32), noise, direction, residual)
    new_residual = residual - alpha * kd
    return (solution + alpha * direction, new_residual, new_residual + beta * direction, norm_sq.reshape(32))


def solution(mesh):
    data = P(None, ("wide", "narrow"))
    return jax.shard_map(
        body,
        mesh=mesh,
        in_specs=(data, P(), P(), data, data, data),
        out_specs=(data, data, data, P()),
        check_vma=False,
    )
```

```python
import functools
import math

import jax
import jax.numpy as jnp
from jax import lax
from jax.experimental import pallas as pl
from jax.experimental.pallas import tpu as pltpu
from jax.sharding import PartitionSpec as P

F32, BF16 = jnp.float32, jnp.bfloat16
MESH = pl.DeviceIdType.MESH
NX, NY, NZ = 4, 4, 16
NPEER = NX * NY
BLK = 192
CHUNK = NY * BLK
HOME = NPEER * BLK
VIS = 2 * BLK
HALF = NZ // 2
COORD_SCALE = math.sqrt(5.0) / 3.0
EXP_SCALE = -3.0 * math.log2(math.e)
EXP_SHIFT = math.log2(3.0)
NT = (((1,), (1,)), ((), ()))


def matern(u):
    u = jnp.maximum(u, 1e-30)
    q = u * lax.rsqrt(u)
    e = jnp.exp2(q * EXP_SCALE + EXP_SHIFT)
    return (((u + q) + (1.0 / 3.0)) * e).astype(BF16)


def pack_tail(tail):
    lane = lax.broadcasted_iota(jnp.int32, (16, 128), 1)
    return jnp.where(lane < 64, tail[0:16], pltpu.roll(tail[16:32], 64, 1))


def pack_high(tail):
    lane = lax.broadcasted_iota(jnp.int32, (16, 128), 1)
    return jnp.where(lane < 64, pltpu.roll(tail[0:16], 64, 1), tail[16:32])


def unpack_tails(a, b):
    lane = lax.broadcasted_iota(jnp.int32, (16, 128), 1)
    top = jnp.where(lane < 64, a, pltpu.roll(b, 64, 1))
    bottom = jnp.where(lane < 64, pltpu.roll(a, 64, 1), b)
    return jnp.concatenate([top, bottom], axis=0)


def unpack(blocks):
    heads = [b[0:32] for b in blocks]
    tails = [unpack_tails(blocks[i][32:48], blocks[i + 1][32:48]) for i in range(0, len(blocks), 2)]
    return jnp.concatenate(heads + tails, axis=1)


def split3(v):
    hi = v.astype(BF16)
    rest = v - hi.astype(F32)
    mid = rest.astype(BF16)
    lo = (rest - mid.astype(F32)).astype(BF16)
    return hi, mid, lo


def norm_rows(s, first):
    sq = jnp.sum(s * s, axis=0, keepdims=True)
    hi, mid, lo = (p.astype(F32) for p in split3(sq))
    row = lax.broadcasted_iota(jnp.int32, (16, s.shape[1]), 0)
    ones = jnp.where(row < 6, 1.0, 0.0)
    rows = jnp.where(row == first, hi, jnp.where(row == first + 1, mid, jnp.where(row == first + 2, lo, ones)))
    return rows.astype(BF16)


def home_operand(s):
    hi, mid, lo = split3(s)
    pad = jnp.zeros((48, s.shape[1]), BF16)
    return jnp.concatenate([hi, hi, mid, mid, hi, lo, norm_rows(s, 0), pad], axis=0)


def visitor_operand(s):
    hi, mid, lo = split3(s)
    hi, mid, lo = (p * BF16(-2.0) for p in (hi, mid, lo))
    pad = jnp.zeros((48, s.shape[1]), BF16)
    return jnp.concatenate([hi, mid, hi, mid, lo, hi, norm_rows(s, 3), pad], axis=0).T


def to_row(cols):
    lane = lax.broadcasted_iota(jnp.int32, (32, 128), 1)
    sub = lax.broadcasted_iota(jnp.int32, (32, 128), 0)
    out = jnp.zeros((32, 128), F32)
    for i, col in enumerate(cols):
        out = jnp.where(lane == sub + 32 * i, col, out)
    return jnp.sum(out, axis=0, keepdims=True)


def to_col(row, i):
    lane = lax.broadcasted_iota(jnp.int32, (32, 128), 1)
    sub = lax.broadcasted_iota(jnp.int32, (32, 128), 0)
    return jnp.sum(jnp.where(lane == sub + 32 * i, row, 0.0), axis=1, keepdims=True)


def kernel(
    pts_hbm, ls_hbm, noise_ref, dir_hbm, res_hbm,
    kd_out, alpha_out, beta_out, ratio_out, rr_out,
    pts_ref, ls_ref, dir_ref, res_ref,
    tail, own_s, own_d, home_s, home_d, vis_s, vis_d, hb, hd, va, vd, hacc, ret, ret_tail, sum_head, sum_tail, red_tail,
    cross_a, cross_b, fin_a, fin_b, red_a, red_b, ar1_src, ar1, ar2_src, ar2,
    in_sem, home_send, home_recv, zs_send, z_recv, sib_send, sib_recv,
    cross_send, cross_recv, fin_send, fin_recv, red_send, red_recv, ar1_send, ar1_recv, ar2_send, ar2_recv,
):
    wide, narrow = lax.axis_index("wide"), lax.axis_index("narrow")
    z, y_hi, core = wide // 4, (wide // 2) % 2, wide % 2
    x, y_lo = narrow // 2, narrow % 2
    y = y_hi * 2 + y_lo

    def peer(dz=0, dx=0, dy=0, dc=0):
        pz, px, py, pc = (z + dz) % NZ, (x + dx) % NX, (y + dy) % NY, (core + dc) % 2
        return (pz * 4 + (py // 2) * 2 + pc, px * 2 + py % 2)

    def remote(src, dst, send, recv, dev):
        return pltpu.make_async_remote_copy(
            src_ref=src, dst_ref=dst, send_sem=send, recv_sem=recv, device_id=dev, device_id_type=MESH
        )

    plane = [(dx, dy) for dx in range(NX) for dy in range(NY)]

    fetches = [
        pltpu.make_async_copy(src, dst, in_sem.at[i])
        for i, (src, dst) in enumerate(((pts_hbm, pts_ref), (ls_hbm, ls_ref), (dir_hbm, dir_ref), (res_hbm, res_ref)))
    ]
    for fetch in fetches:
        fetch.start()

    barrier = pltpu.get_barrier_semaphore()
    senders = [dict(dx=dx, dy=dy) for dx, dy in plane[1:]] + [dict(dz=1), dict(dz=2), dict(dc=1)]
    for sender in senders:
        pl.semaphore_signal(barrier, inc=1, device_id=peer(**sender), device_id_type=MESH)

    for fetch in fetches[:3]:
        fetch.wait()
    eye = lax.broadcasted_iota(jnp.int32, (32, 32), 0) == lax.broadcasted_iota(jnp.int32, (32, 32), 1)
    scale = jnp.sum(jnp.where(eye, ls_ref[...], 0.0), axis=1, keepdims=True)
    scaled = pts_ref[...] / scale * COORD_SCALE
    own_s[0:32] = scaled[:, 0:128]
    tail[...] = jnp.zeros_like(tail)
    tail[:, 0:64] = scaled[:, 128:192]
    own_s[32:48] = pack_tail(tail[...])
    own_d[0:32] = dir_ref[:, 0:128].astype(BF16)
    tail[:, 0:64] = dir_ref[:, 128:192]
    own_d[32:48] = pack_tail(tail[...]).astype(BF16)

    hacc[...] = jnp.zeros_like(hacc)
    ret[...] = jnp.zeros_like(ret)
    pl.semaphore_wait(barrier, len(senders))

    own, vis, home = (own_s, own_d), (vis_s, vis_d), (home_s, home_d)

    def home_copy(dx, dy, slot, which):
        return remote(
            own[which], home[which].at[slot], home_send.at[which, dx * NY + dy], home_recv.at[which, slot], peer(dx=dx, dy=dy)
        )

    def z_copy(k, which):
        src = own[which] if k <= 2 else vis[which].at[k - 2, 0]
        return remote(src, vis[which].at[k, 0], zs_send.at[which, k], z_recv.at[which, k], peer(dz=NZ - min(k, 2)))

    def sib_copy(k, which):
        src = own[which] if k == 0 else vis[which].at[k, 0]
        return remote(src, vis[which].at[k, 1], sib_send.at[which, k], sib_recv.at[which, k], peer(dc=1))

    for which in range(2):
        sib_copy(0, which).start()
    for k in (1, 2):
        for which in range(2):
            z_copy(k, which).start()
    for dx in (0, 1, 3, 2):
        for dy in range(NY):
            if dx or dy:
                for which in range(2):
                    home_copy(dx, dy, ((-dx) % NX) * NY + (-dy) % NY, which).start()

    vis_s[0, 0] = own_s[...]
    vis_d[0, 0] = own_d[...]
    home_s[0] = own_s[...]
    home_d[0] = own_d[...]

    def set_visitors(k, at):
        va[at:at + VIS] = visitor_operand(unpack([vis_s[k, 0], vis_s[k, 1]]))
        vd[:, at:at + VIS] = unpack([vis_d[k, 0].astype(F32), vis_d[k, 1].astype(F32)]).astype(BF16)

    def pass_on(k):
        for which in range(2):
            z_copy(k, which).wait_recv()
        for which in range(2):
            sib_copy(k, which).start()
            if k + 2 <= HALF:
                z_copy(k + 2, which).start()

    def columns(g):
        return pl.ds(pl.multiple_of(g * CHUNK, CHUNK), CHUNK)

    def visitors(k, at):
        for which in range(2):
            sib_copy(k, which).wait_recv()
        set_visitors(k, at)

    def begin():
        for k in (1, 2):
            pass_on(k)
        for k in (1, 2):
            visitors(k, VIS * (k - 1))

    def first(t, carry):
        g = t + (t // 2) * (5 - 2 * t)
        for dy in range(NY):
            for which in range(2):
                copy = home_copy(g, dy, g * NY + dy, which)
                if dy:
                    copy.wait_recv()
                else:
                    pl.when(t > 0)(copy.wait_recv)
        cols = columns(g)
        hb[:, cols] = home_operand(unpack([home_s[g * NY + dy] for dy in range(NY)]))
        hd[:, cols] = unpack([home_d[g * NY + dy].astype(F32) for dy in range(NY)]).astype(BF16)
        pl.when(t == 0)(begin)

        @pl.when(t == 2)
        def _():
            pass_on(3)
            pass_on(4)

        tile = matern(jnp.dot(va[...], hb[:, cols], preferred_element_type=F32))
        hacc[:, cols] += jnp.dot(vd[...], tile, preferred_element_type=F32)
        ret[0] += lax.dot_general(hd[:, cols], tile, NT, preferred_element_type=F32)
        return carry

    lax.fori_loop(0, NX, first, 0)

    def cross_copy(k, part):
        pair, half = (k - 1) // 2, (k - 1) % 2
        src = ret.at[pair, :, pl.ds(VIS * half + 128, 128)] if part == 0 else ret_tail.at[k]
        dst = (cross_a, cross_b)[part].at[k]
        return remote(src, dst, cross_send.at[k, part], cross_recv.at[k, part], peer(dc=1))

    def fin_copy(k, part):
        src, dst = ((sum_head, fin_a), (sum_tail, fin_b))[part]
        return remote(src.at[k], dst.at[k], fin_send.at[k, part], fin_recv.at[k, part], peer(dz=k))

    def exchange(ks):
        for k in ks:
            pair, half = (k - 1) // 2, (k - 1) % 2
            ret_tail[k] = pack_high(ret[pair, :, pl.ds(VIS * half + 256, 128)])
            for part in range(2):
                cross_copy(k, part).start()

    def send_home(ks):
        for k in ks:
            pair, half = (k - 1) // 2, (k - 1) % 2
            for part in range(2):
                cross_copy(k, part).wait_recv()
            sum_head[k] = ret[pair, :, pl.ds(VIS * half, 128)] + cross_a[k]
            sum_tail[k] = pack_tail(ret[pair, :, pl.ds(VIS * half + 256, 128)]) + cross_b[k]
            for part in range(2):
                fin_copy(k, part).start()

    exchange((1, 2))

    for pair in (1, 2):
        visitors(2 * pair + 1, 0)
        visitors(2 * pair + 2, VIS)

        def both(g, carry, pair=pair):
            cols = columns(g)
            tile = matern(jnp.dot(va[...], hb[:, cols], preferred_element_type=F32))
            hacc[:, cols] += jnp.dot(vd[...], tile, preferred_element_type=F32)
            ret[pair] += lax.dot_general(hd[:, cols], tile, NT, preferred_element_type=F32)

            @pl.when(g == 1)
            def _():
                pass_on(2 * pair + 3)
                pass_on(2 * pair + 4)
                send_home((2 * pair - 1, 2 * pair))

            return carry

        lax.fori_loop(0, NX, both, 0)
        exchange((2 * pair + 1, 2 * pair + 2))

    visitors(7, 0)

    def seventh(g, carry):
        cols = columns(g)
        tile = matern(jnp.dot(va[0:VIS], hb[:, cols], preferred_element_type=F32))
        hacc[:, cols] += jnp.dot(vd[:, 0:VIS], tile, preferred_element_type=F32)
        ret[3, :, 0:VIS] += lax.dot_general(hd[:, cols], tile, NT, preferred_element_type=F32)
        pl.when(g == 1)(functools.partial(send_home, (5, 6)))
        return carry

    lax.fori_loop(0, NX, seventh, 0)
    exchange((7,))

    visitors(8, 0)
    visitors(0, VIS)
    def red_copy(dx, dy, slot, part):
        base = dx * CHUNK + 128 * dy
        src = hacc.at[:, pl.ds(pl.multiple_of(base, 128), 128)] if part == 0 else red_tail.at[dx * NY + dy]
        dst = (red_a, red_b)[part].at[slot]
        return remote(src, dst, red_send.at[part, dx * NY + dy], red_recv.at[part, slot], peer(dx=dx, dy=dy))

    def back(dx, dy):
        return ((NX - dx) % NX) * NY + (NY - dy) % NY

    def last_pair(t, carry):
        g = (t + 1) % NX
        cols = columns(g)
        tile = matern(jnp.dot(va[...], hb[:, cols], preferred_element_type=F32))
        hacc[:, cols] += jnp.dot(vd[...], tile, preferred_element_type=F32)
        for dy in range(NY):
            tails = hacc[:, pl.ds(pl.multiple_of(g * CHUNK + 512 + 128 * (dy // 2), 128), 128)]
            red_tail[g * NY + dy] = pack_high(tails) if dy % 2 else pack_tail(tails)

        def send(dy):
            for part in range(2):
                red_copy(g, dy, back(g, dy), part).start()

        for dy in range(1, NY):
            send(dy)
        pl.when(g > 0)(functools.partial(send, 0))
        pl.when(t == 0)(functools.partial(send_home, (7,)))
        return carry

    lax.fori_loop(0, NX, last_pair, 0)

    fetches[3].wait()
    direction = dir_ref[...]
    residual = res_ref[...]
    sum_a, sum_b = hacc[:, 0:128], red_tail[0]
    for dx, dy in plane[1:]:
        for part in range(2):
            red_copy(dx, dy, dx * NY + dy, part).wait_recv()
        sum_a = sum_a + red_a[dx * NY + dy]
        sum_b = sum_b + red_b[dx * NY + dy]
    for k in range(1, HALF):
        for part in range(2):
            fin_copy(k, part).wait_recv()
        sum_a = sum_a + fin_a[k]
        sum_b = sum_b + fin_b[k]
    last_points = jnp.concatenate([sum_b, pltpu.roll(sum_b, 64, 1)], axis=0)[:, 0:64]
    kd = jnp.concatenate([sum_a, last_points], axis=1) + noise_ref[0] * direction
    kd_out[...] = kd

    def total(v):
        return jnp.sum(v, axis=1, keepdims=True)

    sums = to_row([total(residual * residual), total(direction * kd), total(residual * kd), total(kd * kd)])

    ar1_src[...] = sums
    me1 = (x * NY + y) * 2 + core
    near = [(dx, dy, dc) for dx, dy in plane for dc in range(2)][1:]

    def ar1_copy(dx, dy, dc, slot):
        i = (dx * NY + dy) * 2 + dc
        return remote(ar1_src, ar1.at[slot], ar1_send.at[i], ar1_recv.at[slot], peer(dx=dx, dy=dy, dc=dc))

    for dx, dy, dc in near:
        ar1_copy(dx, dy, dc, me1).start()
    ar1[me1] = sums
    for which in range(2):
        for pos in range(HALF + 1):
            if pos:
                z_copy(pos, which).wait_send()
            sib_copy(pos, which).wait_send()
        for dx, dy in plane[1:]:
            home_copy(dx, dy, dx * NY + dy, which).wait_send()
            red_copy(dx, dy, dx * NY + dy, which).wait_send()
    for k in range(1, HALF):
        for part in range(2):
            cross_copy(k, part).wait_send()
            fin_copy(k, part).wait_send()
    for dx, dy, dc in near:
        ar1_copy(dx, dy, dc, (((x + dx) % NX) * NY + (y + dy) % NY) * 2 + (core + dc) % 2).wait_recv()
    acc = jnp.sum(ar1[...], axis=0)
    ar2_src[...] = acc

    def ar2_copy(dz, slot):
        return remote(ar2_src, ar2.at[slot], ar2_send.at[dz], ar2_recv.at[slot], peer(dz=dz))

    for dz in range(1, NZ):
        ar2_copy(dz, z).start()
    ar2[z] = acc
    for dz in range(1, NZ):
        ar2_copy(dz, (z + dz) % NZ).wait_recv()
    acc = jnp.sum(ar2[...], axis=0)

    rr, curve, r_kd, kd_sq = (to_col(acc, i) for i in range(4))
    alpha = rr / curve
    norm_sq = rr - 2.0 * alpha * r_kd + alpha * alpha * kd_sq
    alpha_out[...] = jnp.broadcast_to(alpha, (32, BLK))
    beta_out[...] = jnp.broadcast_to(norm_sq / rr, (32, BLK))
    ratio_out[...] = jnp.sum(jnp.where(eye, norm_sq / rr, 0.0), axis=0)
    rr_out[...] = jnp.sum(jnp.where(eye, rr, 0.0), axis=0)

    for dx, dy, dc in near:
        ar1_copy(dx, dy, dc, me1).wait_send()
    for dz in range(1, NZ):
        ar2_copy(dz, z).wait_send()


def body(points, lengthscale, noise, direction, residual, solution):
    vmem, smem = pl.BlockSpec(memory_space=pltpu.VMEM), pl.BlockSpec(memory_space=pltpu.SMEM)
    hbm = pl.BlockSpec(memory_space=pl.ANY)
    dma = pltpu.SemaphoreType.DMA
    block = jax.ShapeDtypeStruct((32, BLK), F32)
    row = jax.ShapeDtypeStruct((32,), F32)
    kd, alpha, beta, ratio, rr = pl.pallas_call(
        kernel,
        out_shape=[block, block, block, row, row],
        in_specs=[hbm, hbm, smem, hbm, hbm],
        out_specs=[vmem] * 5,
        scratch_shapes=[
            pltpu.VMEM((32, BLK), F32),
            pltpu.VMEM((1, 32), F32),
            pltpu.VMEM((32, BLK), F32),
            pltpu.VMEM((32, BLK), F32),
            pltpu.VMEM((32, 128), F32),
            pltpu.VMEM((48, 128), F32),
            pltpu.VMEM((48, 128), BF16),
            pltpu.VMEM((NPEER, 48, 128), F32),
            pltpu.VMEM((NPEER, 48, 128), BF16),
            pltpu.VMEM((HALF + 1, 2, 48, 128), F32),
            pltpu.VMEM((HALF + 1, 2, 48, 128), BF16),
            pltpu.VMEM((256, HOME), BF16),
            pltpu.VMEM((32, HOME), BF16),
            pltpu.VMEM((2 * VIS, 256), BF16),
            pltpu.VMEM((32, 2 * VIS), BF16),
            pltpu.VMEM((32, HOME), F32),
            pltpu.VMEM((HALF // 2, 32, 2 * VIS), F32),
            pltpu.VMEM((HALF, 16, 128), F32),
            pltpu.VMEM((HALF, 32, 128), F32),
            pltpu.VMEM((HALF, 16, 128), F32),
            pltpu.VMEM((NPEER, 16, 128), F32),
            pltpu.VMEM((HALF, 32, 128), F32),
            pltpu.VMEM((HALF, 16, 128), F32),
            pltpu.VMEM((HALF, 32, 128), F32),
            pltpu.VMEM((HALF, 16, 128), F32),
            pltpu.VMEM((NPEER, 32, 128), F32),
            pltpu.VMEM((NPEER, 16, 128), F32),
            pltpu.VMEM((1, 128), F32),
            pltpu.VMEM((2 * NPEER, 1, 128), F32),
            pltpu.VMEM((1, 128), F32),
            pltpu.VMEM((NZ, 1, 128), F32),
            dma((4,)),
            dma((2, NPEER)), dma((2, NPEER)),
            dma((2, HALF + 1)), dma((2, HALF + 1)),
            dma((2, HALF + 1)), dma((2, HALF + 1)),
            dma((HALF, 2)), dma((HALF, 2)),
            dma((HALF, 2)), dma((HALF, 2)),
            dma((2, NPEER)), dma((2, NPEER)),
            dma((2 * NPEER,)), dma((2 * NPEER,)),
            dma((NZ,)), dma((NZ,)),
        ],
        compiler_params=pltpu.CompilerParams(
            collective_id=0, has_side_effects=True, vmem_limit_bytes=63 * 1024 * 1024
        ),
    )(points, lengthscale.reshape(1, 32), noise, direction, residual)
    new_residual = residual - alpha * kd
    return (solution + alpha * direction, new_residual, new_residual + beta * direction, ratio * rr)


def solution(mesh):
    data = P(None, ("wide", "narrow"))
    return jax.shard_map(
        body,
        mesh=mesh,
        in_specs=(data, P(), P(), data, data, data),
        out_specs=(data, data, data, P()),
        check_vma=False,
    )
```
